32 devices in a mesh: tm: 4 (over y, x), rows: 4 (over z), dp: 2 (over core).
Axes of the slice: x: 2, y: 2, z: 4, core: 2. Of those that a mesh axis runs over, the one named last changes fastest.
Arguments:
- latent_grad: bfloat16 [18432, 64], P(('dp', 'tm'), 'rows'), parts along dimension 0, may hold values from -6 to 6
- features: bfloat16 [16, 48, 96, 384], P(('dp', 'tm'), 'rows'), parts along dimension 0, may hold values from -6 to 6
- head_weight: bfloat16 [432, 384], replicated, may hold values from -0.0625 to 0.0625
Outputs:
- grad_features: bfloat16 [16, 48, 96, 384], P(('dp', 'tm'), 'rows'), parts along dimension 0
- head_weight_grad: float32 [864, 384], P('dp'), parts along dimension 0
The draws below stay inside these ranges and needn't reach their ends.
There are 2 independent parts, one for each index of `dp`. The reference program is written for one: setup_inputs(seed, part) draws one part's arguments, and reference() takes and returns one part's arrays. A program takes and returns all parts, laid end to end along the dimension named above; an argument that names none is the same for every part. Nothing has to cross between parts.
All inputs are finite; a program needn't handle non-finite values.
Results may differ from the reference program's by a relative error of at most 0.0031.
Values may be sent and summed in bfloat16 or wider, within the bound.
No kernel may reach another device: no remote copies, remote signals or barrier semaphores. Data moves between devices by JAX's collectives and lax.ppermute only.
A program may use at most 64 MiB of HBM per device.

```python
import math
import jax
import jax.numpy as jnp
from jax import lax

C = 384
CL = 16
W = 96
NT = 8
NH = 48
FEAT = 64
TOKENS = 9216
TOK_TM = 2304
N_TM = 4


def block_scale(own_key, extent, cuts, low, high):
    factor_of, own = 1.0, jax.random.fold_in(own_key, 6)
    for axis_at, shards_of in cuts:
        draws = jnp.exp(jax.random.uniform(jax.random.fold_in(own, axis_at), (shards_of,), jnp.float32, low / len(cuts), high / len(cuts)))
        factor_of = factor_of * jnp.repeat(draws, extent[axis_at] // shards_of).reshape([-1 if axis == axis_at else 1 for axis in range(len(extent))])
    return factor_of


def noise(key, shape, spread, reach, shards=(), kind=jnp.bfloat16):
    loudness = block_scale(key, shape, shards, -0.22, 0.18) if shards else 1.0
    values = jax.random.normal(key, shape, jnp.float32) * spread * loudness
    return jnp.minimum(jnp.maximum(values, -reach), reach).astype(kind)


def setup_inputs(seed: int = 0, part: int = 0) -> dict:
    seeds = jax.random.split(jax.random.key(seed), 4)
    part_keys = jax.random.split(jax.random.fold_in(seeds[3], part), 4)
    return {
        "latent_grad": noise(part_keys[0], (TOKENS, FEAT), 1.0, 6.0, ((0, 4), (1, 4))),
        "features": noise(part_keys[1], (NT, NH, W, C), 1.0, 6.0, ((0, 4), (1, 4))),
        "head_weight": noise(seeds[2], (27 * CL, C), (27 * C) ** -0.5, 0.0625),
    }


def to_grid(latent_grad):
    split = latent_grad.reshape(N_TM, TOK_TM // 2, 2, FEAT)
    first = split[:, :, 0]
    second = split[::-1, :, 1]
    ordered = jnp.concatenate([first, second], axis=0)
    ordered = ordered.transpose(1, 0, 2).reshape(TOKENS, FEAT)
    grid = ordered.reshape(NT, NH // 2, W // 2, CL, 2, 2)
    return grid.transpose(0, 1, 4, 2, 5, 3).reshape(NT, NH, W, CL)

def reference(latent_grad, features, head_weight):
    grid = to_grid(latent_grad)
    padded = jnp.pad(grid, ((0, 2), (1, 1), (1, 1), (0, 0)))

    def frame_step(total, frame):
        window = lax.dynamic_slice_in_dim(padded, frame, 3, 0)
        pieces = []
        for kt in range(3):
            for kh in range(3):
                for kw in range(3):
                    pieces.append(window[2 - kt, 2 - kh:2 - kh + NH, 2 - kw:2 - kw + W, :])
        cols = jnp.concatenate(pieces, axis=-1).reshape(NH * W, 27 * CL)
        hidden = lax.dynamic_index_in_dim(features, frame, 0, keepdims=False).reshape(NH * W, C).astype(jnp.float32)
        sig = jax.nn.sigmoid(hidden)
        act = (hidden * sig).astype(jnp.bfloat16)
        pre = jnp.dot(cols, head_weight, preferred_element_type=jnp.float32)
        grads = (pre * sig * (1.0 + hidden * (1.0 - sig))).astype(jnp.bfloat16)
        term = lax.dot_general(cols, act, (((0,), (0,)), ((), ())), preferred_element_type=jnp.float32)
        return (total + term, grads.reshape(NH, W, C))
    start = jnp.zeros((27 * CL, C), jnp.float32)
    total, grad_features = lax.scan(frame_step, start, jnp.arange(NT, dtype=jnp.int32))
    scale = 1.0 / math.sqrt(NT * NH * W)
    return (grad_features, total * scale)
```

```python
import functools
import math

import jax
import jax.numpy as jnp
import numpy as np
from jax import lax
from jax.experimental import pallas as pl
from jax.experimental.pallas import tpu as pltpu
from jax.sharding import PartitionSpec as P

LANES = 128
TAPS = 27


class Sizes:
    def __init__(self, n_time, n_rows, latent_shape, features_shape):
        self.n_time, self.n_rows = n_time, n_rows
        self.frames, self.rows, self.width, self.channels = features_shape
        self.tokens, self.feat = latent_shape
        self.latent = self.feat * n_rows // 4
        self.cycle = 2 * n_time
        self.row_tokens = self.width // 2
        self.band = self.rows // 2
        self.band_x = self.band + 2
        self.frames_x = self.frames + 2
        self.all_frames = self.frames * n_time
        self.band_cycles = self.band * self.row_tokens // self.cycle
        self.halo_cycles = -(-self.row_tokens // self.cycle)
        self.halo = 2 * self.halo_cycles
        self.lanes = 2 * self.band_cycles + 2 * self.halo
        self.sources = n_time * n_rows
        self.grid_rows = self.frames * self.rows
        self.piece_taps = -(-TAPS // n_time)
        self.piece = self.piece_taps * self.latent
        self.cols = self.piece * n_time


def sort_rows(z):
    count = z.n_rows * z.frames_x * z.feat
    out = np.zeros((count, count), np.float32)
    part = z.feat // 4
    for r in range(z.n_rows):
        for t in range(z.frames_x):
            for e in range(part):
                for p in range(2):
                    for q in range(2):
                        source = (r * z.frames_x + t) * z.feat + 4 * e + 2 * p + q
                        target = ((q * 2 + p) * z.frames_x + t) * z.latent + r * part + e
                        out[target, source] = 1
    return jnp.asarray(out, jnp.bfloat16)


def place_lanes(z):
    out = np.zeros((2, z.n_time, LANES, z.band_x, LANES), np.float32)
    for q in range(2):
        for i in range(z.n_time):
            for lane in range(z.lanes):
                place = z.cycle - 1 - i if lane % 2 else i
                token = (lane // 2 - z.halo_cycles) * z.cycle + place + z.row_tokens
                if 0 <= token < z.band_x * z.row_tokens:
                    out[q, i, lane, token // z.row_tokens, 2 * (token % z.row_tokens) + q] = 1
    return jnp.asarray(out.reshape(2 * z.n_time * LANES, z.band_x * LANES), jnp.bfloat16)


def pack_kernel(z, latent_ref, out_ref):
    tiles = z.tokens // LANES
    zero = jnp.zeros((z.feat, LANES), jnp.float32)
    lane = lax.broadcasted_iota(jnp.int32, (z.feat, LANES), 1)

    def tile(index):
        if index < 0 or index >= tiles:
            return zero
        return latent_ref[:, index * LANES : (index + 1) * LANES].astype(jnp.float32)

    def window(t, r):
        start = 2 * (t * z.n_rows + r) * z.band_cycles - z.halo
        first, offset = start // LANES, start % LANES
        value = tile(first)
        if offset:
            value = jnp.concatenate([value, tile(first + 1)], axis=1)
            value = pltpu.roll(value, 2 * LANES - offset, 1)[:, :LANES]
        low = z.halo if r == 0 else 0
        high = z.lanes - z.halo if r == z.n_rows - 1 else z.lanes
        return jnp.where((lane >= low) & (lane < high), value, 0.0)

    for r in range(z.n_rows):
        held = [window(t, r) for t in range(z.all_frames)] + [zero, zero]
        for i in range(z.n_time):
            block = jnp.concatenate(held[i * z.frames : i * z.frames + z.frames_x], axis=0)
            out_ref[i * z.n_rows + r] = block.astype(jnp.bfloat16)


def fill_cols(z, moved_ref, sort_ref, place_ref, cols_ref):
    rows = z.n_rows * z.frames_x * z.feat
    moved = [moved_ref[i * z.n_rows : (i + 1) * z.n_rows].reshape(rows, LANES) for i in range(z.n_time)]
    ordered = jnp.dot(
        sort_ref[...], jnp.concatenate(moved, axis=1), preferred_element_type=jnp.float32
    ).astype(jnp.bfloat16)
    half = rows // 2
    pair = jnp.concatenate([ordered[:half], ordered[half:]], axis=1)
    grid = jnp.dot(pair, place_ref[...], preferred_element_type=jnp.float32)
    for a in range(z.band_x):
        block = grid[:, a * LANES : (a + 1) * LANES]
        for kw in range(3):
            turned = block if kw == 1 else pltpu.roll(block, LANES - 1 if kw == 0 else 1, 1)
            turned = turned.astype(jnp.bfloat16)
            for p in range(2):
                for t in range(z.frames_x):
                    at = (p * z.frames_x + t) * z.latent
                    value = turned[at : at + z.latent]
                    for kt in range(3):
                        for kh in range(3):
                            frame, row = t - 2 + kt, 2 * (a - 1) + p - 1 + kh
                            if 0 <= frame < z.frames and 0 <= row < z.rows:
                                tap = ((kt * 3 + kh) * 3 + kw) * z.latent
                                lane = (frame * z.rows + row) * LANES
                                cols_ref[tap : tap + z.latent, lane : lane + LANES] = value
    if z.cols > TAPS * z.latent:
        shape = (z.cols - TAPS * z.latent, z.grid_rows * LANES)
        cols_ref[TAPS * z.latent :, :] = jnp.zeros(shape, jnp.bfloat16)


def weight_kernel(z, moved_ref, sort_ref, place_ref, features_ref, *refs):
    own_ref, other_refs, (cols_ref, act_ref, total_ref) = refs[0], refs[1 : z.n_time], refs[z.n_time :]
    for row in range(z.grid_rows):
        hidden = features_ref[row * z.width : (row + 1) * z.width, :].astype(jnp.float32)
        act = hidden * (0.5 + 0.5 * jnp.tanh(0.5 * hidden))
        act_ref[row * LANES : row * LANES + z.width, :] = act.astype(jnp.bfloat16)
        shape = (LANES - z.width, z.channels)
        act_ref[row * LANES + z.width : (row + 1) * LANES, :] = jnp.zeros(shape, jnp.bfloat16)
    fill_cols(z, moved_ref, sort_ref, place_ref, cols_ref)
    total_ref[...] = jnp.dot(cols_ref[...], act_ref[...], preferred_element_type=jnp.float32)
    me = lax.axis_index("tm")
    for step in range(z.n_time):
        start = pl.multiple_of((me ^ step) * z.piece, z.piece)
        value = total_ref[pl.ds(start, z.piece), :]
        if step == 0:
            own_ref[...] = value
        else:
            other_refs[step - 1][...] = value.astype(jnp.bfloat16)


def features_kernel(z, moved_ref, sort_ref, place_ref, features_ref, weight_ref, out_ref, cols_ref):
    fill_cols(z, moved_ref, sort_ref, place_ref, cols_ref)
    step = 4
    for first in range(0, z.grid_rows, step):
        count = min(step, z.grid_rows - first)
        part = cols_ref[: TAPS * z.latent, first * LANES : (first + count) * LANES]
        product = lax.dot_general(
            part, weight_ref[...], (((0,), (0,)), ((), ())), preferred_element_type=jnp.float32
        )
        for k in range(count):
            row = first + k
            hidden = features_ref[row * z.width : (row + 1) * z.width, :].astype(jnp.float32)
            sig = 0.5 + 0.5 * jnp.tanh(0.5 * hidden)
            value = product[k * LANES : k * LANES + z.width] * sig * (1.0 + hidden * (1.0 - sig))
            out_ref[row * z.width : (row + 1) * z.width, :] = value.astype(jnp.bfloat16)


def join_kernel(z, *refs):
    piece_refs, out_ref, held_ref = refs[: z.n_time], refs[z.n_time], refs[z.n_time + 1]
    me = lax.axis_index("tm")
    for step, ref in enumerate(piece_refs):
        start = pl.multiple_of((me ^ step) * z.piece, z.piece)
        held_ref[pl.ds(start, z.piece), :] = ref[...].astype(jnp.float32)
    out_ref[...] = held_ref[: TAPS * z.latent, :]


def exchange(values, axis):
    size = lax.axis_size(axis)
    return [
        lax.ppermute(value, axis, [(i, i ^ step) for i in range(size)])
        for step, value in enumerate(values, 1)
    ]


def tree_sum(values):
    while len(values) > 1:
        values = [values[i] + values[i + 1] for i in range(0, len(values), 2)]
    return values[0]


def shards(latent_grad, features, head_weight):
    n_time, n_rows = lax.axis_size("tm"), lax.axis_size("rows")
    z = Sizes(n_time, n_rows, latent_grad.shape, features.shape)
    params = pltpu.CompilerParams(vmem_limit_bytes=32 * 1024 * 1024)
    f32, bf16 = jnp.float32, jnp.bfloat16
    cells = z.grid_rows * z.width
    packed = pl.pallas_call(
        functools.partial(pack_kernel, z),
        out_shape=jax.ShapeDtypeStruct((z.sources, z.frames_x * z.feat, LANES), bf16),
        compiler_params=params,
        name="pack_latents",
    )(latent_grad.T)
    moved = lax.all_to_all(packed, ("tm", "rows"), 0, 0, tiled=True)
    sort, place = sort_rows(z), place_lanes(z)
    flat = features.reshape(cells, z.channels)
    cols_scratch = pltpu.VMEM((z.cols, z.grid_rows * LANES), bf16)
    products = z.cols * z.grid_rows * LANES * z.channels
    pieces = pl.pallas_call(
        functools.partial(weight_kernel, z),
        out_shape=[
            jax.ShapeDtypeStruct((z.piece, z.channels), bf16 if s else f32) for s in range(n_time)
        ],
        scratch_shapes=[
            cols_scratch,
            pltpu.VMEM((z.grid_rows * LANES, z.channels), bf16),
            pltpu.VMEM((z.cols, z.channels), f32),
        ],
        compiler_params=params,
        cost_estimate=pl.CostEstimate(
            flops=2 * products, bytes_accessed=2 * cells * z.channels, transcendentals=cells * z.channels
        ),
        name="weight_term",
    )(moved, sort, place, flat)
    grad = pl.pallas_call(
        functools.partial(features_kernel, z),
        out_shape=jax.ShapeDtypeStruct((cells, z.channels), bf16),
        scratch_shapes=[cols_scratch],
        compiler_params=params,
        cost_estimate=pl.CostEstimate(
            flops=2 * products, bytes_accessed=4 * cells * z.channels, transcendentals=cells * z.channels
        ),
        name="features_grad",
    )(moved, sort, place, flat, head_weight)
    arrived = exchange(pieces[1:], "tm")
    mine = tree_sum([pieces[0]] + [value.astype(f32) for value in arrived]).astype(bf16)
    arrived = exchange([mine] * (n_rows - 1), "rows")
    whole = tree_sum([value.astype(f32) for value in [mine] + arrived])
    scale = 1.0 / math.sqrt(cells * n_time * n_rows)
    whole = (whole * scale).astype(bf16)
    arrived = exchange([whole] * (n_time - 1), "tm")
    weight_grad = pl.pallas_call(
        functools.partial(join_kernel, z),
        out_shape=jax.ShapeDtypeStruct((TAPS * z.latent, z.channels), f32),
        scratch_shapes=[pltpu.VMEM((z.cols, z.channels), f32)],
        compiler_params=params,
        name="join_pieces",
    )(whole, *arrived)
    return (grad.reshape(features.shape), weight_grad)


def solution(mesh):
    return jax.shard_map(
        shards,
        mesh=mesh,
        in_specs=(P(("dp", "tm"), "rows"), P(("dp", "tm"), "rows", None, None), P()),
        out_specs=(P(("dp", "tm"), "rows", None, None), P("dp", None)),
        check_vma=False,
    )
```

```python
import functools
import math

import jax
import jax.numpy as jnp
import numpy as np
from jax import lax
from jax.experimental import pallas as pl
from jax.experimental.pallas import tpu as pltpu
from jax.sharding import PartitionSpec as P

LANES = 128
TAPS = 27


class Sizes:
    def __init__(self, n_time, n_rows, latent_shape, features_shape):
        self.n_time, self.n_rows = n_time, n_rows
        self.frames, self.rows, self.width, self.channels = features_shape
        self.tokens, self.feat = latent_shape
        self.latent = self.feat * n_rows // 4
        self.cycle = 2 * n_time
        self.row_tokens = self.width // 2
        self.band = self.rows // 2
        self.band_x = self.band + 2
        self.frames_x = self.frames + 2
        self.all_frames = self.frames * n_time
        self.band_cycles = self.band * self.row_tokens // self.cycle
        self.halo_cycles = -(-self.row_tokens // self.cycle)
        self.halo = 2 * self.halo_cycles
        self.lanes = 2 * self.band_cycles + 2 * self.halo
        self.sources = n_time * n_rows
        self.grid_rows = self.frames * self.rows
        self.piece_taps = -(-TAPS // n_time)
        self.piece = self.piece_taps * self.latent
        self.cols = self.piece * n_time


def sort_rows(z):
    count = z.n_rows * z.frames_x * z.feat
    out = np.zeros((count, count), np.float32)
    part = z.feat // 4
    for r in range(z.n_rows):
        for t in range(z.frames_x):
            for e in range(part):
                for p in range(2):
                    for q in range(2):
                        source = (r * z.frames_x + t) * z.feat + 4 * e + 2 * p + q
                        target = ((q * 2 + p) * z.frames_x + t) * z.latent + r * part + e
                        out[target, source] = 1
    return jnp.asarray(out, jnp.bfloat16)


def place_lanes(z):
    out = np.zeros((2, z.n_time, LANES, z.band_x, LANES), np.float32)
    for q in range(2):
        for i in range(z.n_time):
            for lane in range(z.lanes):
                place = z.cycle - 1 - i if lane % 2 else i
                token = (lane // 2 - z.halo_cycles) * z.cycle + place + z.row_tokens
                if 0 <= token < z.band_x * z.row_tokens:
                    out[q, i, lane, token // z.row_tokens, 2 * (token % z.row_tokens) + q] = 1
    return jnp.asarray(out.reshape(2 * z.n_time * LANES, z.band_x * LANES), jnp.bfloat16)


def window_kernel(z, source_ref, *refs):
    out_refs, tokens_ref, sem = refs[:-2], refs[-2], refs[-1]
    load = pltpu.make_async_copy(source_ref, tokens_ref, sem)
    load.start()
    load.wait()
    band = lax.axis_index("rows")
    lane = lax.broadcasted_iota(jnp.int32, (z.feat, LANES), 1)
    last = z.tokens // LANES - 2
    for step, out_ref in enumerate(out_refs):
        r = lax.rem(band + step, z.n_rows)
        low = jnp.where(r == 0, z.halo, 0)
        high = jnp.where(r == z.n_rows - 1, z.lanes - z.halo, z.lanes)
        inside = (lane >= low) & (lane < high)
        held = []
        for t in range(z.all_frames):
            start = 2 * (t * z.n_rows + r) * z.band_cycles - z.halo
            tile = jnp.clip(start >> 7, 0, last)
            turn = (2 * LANES - (start - tile * LANES)) & (2 * LANES - 1)
            value = tokens_ref[:, pl.ds(pl.multiple_of(tile * LANES, LANES), 2 * LANES)]
            value = pltpu.roll(value.astype(jnp.float32), turn, 1)[:, :LANES]
            held.append(jnp.where(inside, value, 0.0))
        out_ref[...] = jnp.concatenate(held, axis=0).astype(jnp.bfloat16)


def frames_kernel(z, *refs):
    band_refs, out_refs = refs[: z.n_rows], refs[z.n_rows :]
    time, band = lax.axis_index("tm"), lax.axis_index("rows")
    own, later = z.frames * z.feat, 2 * z.feat
    for step, out_ref in enumerate(out_refs):
        i = time ^ step
        after = jnp.minimum((i + 1) * z.frames, z.all_frames - 2) * z.feat
        for back, ref in enumerate(band_refs):
            r = lax.rem(band + z.n_rows - back, z.n_rows)
            out_ref[r, :own] = ref[pl.ds(pl.multiple_of(i * own, own), own)]
            value = ref[pl.ds(pl.multiple_of(after, later), later)]
            out_ref[r, own:] = jnp.where(i < z.n_time - 1, value, jnp.zeros_like(value))


def prepare_kernel(z, features_ref, sort_ref, place_ref, act_ref, slope_ref, sort_out, place_out, held_ref, sems):
    cells = z.rows * z.width
    frames = [slice(t * cells, (t + 1) * cells) for t in range(z.frames)]
    loads = [
        pltpu.make_async_copy(features_ref.at[here], held_ref.at[here], sems.at[2 + t])
        for t, here in enumerate(frames)
    ]
    copies = [
        pltpu.make_async_copy(sort_ref, sort_out, sems.at[0]),
        pltpu.make_async_copy(place_ref, place_out, sems.at[1]),
    ]
    for copy in loads + copies:
        copy.start()
    for row in range(z.grid_rows):
        if row % z.rows == 0:
            loads[row // z.rows].wait()
        here = slice(row * z.width, (row + 1) * z.width)
        hidden = held_ref[here, :].astype(jnp.float32)
        sig = 0.5 + 0.5 * jnp.tanh(0.5 * hidden)
        act = hidden * sig
        act_ref[row * LANES : row * LANES + z.width, :] = act.astype(jnp.bfloat16)
        shape = (LANES - z.width, z.channels)
        act_ref[row * LANES + z.width : (row + 1) * LANES, :] = jnp.zeros(shape, jnp.bfloat16)
        slope_ref[here, :] = sig * (1.0 + hidden * (1.0 - sig))
    for copy in copies:
        copy.wait()


def fill_cols(z, moved_refs, sort_ref, place_ref, cols_ref, held_ref):
    rows = z.n_rows * z.frames_x * z.feat
    time = lax.axis_index("tm")
    for step, ref in enumerate(moved_refs):
        start = pl.multiple_of((time ^ step) * LANES, LANES)
        held_ref[:, pl.ds(start, LANES)] = ref[...].reshape(rows, LANES)
    ordered = jnp.dot(
        sort_ref[...], held_ref[...], preferred_element_type=jnp.float32
    ).astype(jnp.bfloat16)
    half = rows // 2
    pair = jnp.concatenate([ordered[:half], ordered[half:]], axis=1)
    grid = jnp.dot(pair, place_ref[...], preferred_element_type=jnp.float32)
    for a in range(z.band_x):
        block = grid[:, a * LANES : (a + 1) * LANES]
        for kw in range(3):
            turned = block if kw == 1 else pltpu.roll(block, LANES - 1 if kw == 0 else 1, 1)
            turned = turned.astype(jnp.bfloat16)
            for p in range(2):
                for t in range(z.frames_x):
                    at = (p * z.frames_x + t) * z.latent
                    value = turned[at : at + z.latent]
                    for kt in range(3):
                        for kh in range(3):
                            frame, row = t - 2 + kt, 2 * (a - 1) + p - 1 + kh
                            if 0 <= frame < z.frames and 0 <= row < z.rows:
                                tap = ((kt * 3 + kh) * 3 + kw) * z.latent
                                lane = (frame * z.rows + row) * LANES
                                cols_ref[tap : tap + z.latent, lane : lane + LANES] = value
    if z.cols > TAPS * z.latent:
        shape = (z.cols - TAPS * z.latent, z.grid_rows * LANES)
        cols_ref[TAPS * z.latent :, :] = jnp.zeros(shape, jnp.bfloat16)


def weight_kernel(z, *refs):
    moved_refs, (sort_ref, place_ref, act_ref) = refs[: z.n_time], refs[z.n_time : z.n_time + 3]
    own_ref, other_refs = refs[z.n_time + 3], refs[z.n_time + 4 : -3]
    cols_ref, held_ref, total_ref = refs[-3:]
    fill_cols(z, moved_refs, sort_ref, place_ref, cols_ref, held_ref)
    total_ref[...] = jnp.dot(cols_ref[...], act_ref[...], preferred_element_type=jnp.float32)
    me = lax.axis_index("tm")
    for step in range(z.n_time):
        start = pl.multiple_of((me ^ step) * z.piece, z.piece)
        value = total_ref[pl.ds(start, z.piece), :]
        if step == 0:
            own_ref[...] = value
        else:
            other_refs[step - 1][...] = value.astype(jnp.bfloat16)


def features_kernel(z, cols_ref, slope_ref, weight_ref, out_ref):
    step = 4
    for first in range(0, z.grid_rows, step):
        count = min(step, z.grid_rows - first)
        part = cols_ref[: TAPS * z.latent, first * LANES : (first + count) * LANES]
        product = lax.dot_general(
            part, weight_ref[...], (((0,), (0,)), ((), ())), preferred_element_type=jnp.float32
        )
        for k in range(count):
            here = slice((first + k) * z.width, (first + k + 1) * z.width)
            value = product[k * LANES : k * LANES + z.width] * slope_ref[here, :]
            out_ref[here, :] = value.astype(jnp.bfloat16)


def join_kernel(z, *refs):
    piece_refs, out_ref, held_ref = refs[: z.n_time], refs[z.n_time], refs[z.n_time + 1]
    me = lax.axis_index("tm")
    for step, ref in enumerate(piece_refs):
        start = pl.multiple_of((me ^ step) * z.piece, z.piece)
        held_ref[pl.ds(start, z.piece), :] = ref[...].astype(jnp.float32)
    out_ref[...] = held_ref[: TAPS * z.latent, :]


def in_hbm(value):
    return pltpu.with_memory_space_constraint(value, pltpu.HBM)


def exchange(values, axis):
    size = lax.axis_size(axis)
    return [
        lax.ppermute(value, axis, [(i, i ^ step) for i in range(size)])
        for step, value in enumerate(values, 1)
    ]


def rotate(values, axis):
    size = lax.axis_size(axis)
    return [
        lax.ppermute(value, axis, [(i, (i + step) % size) for i in range(size)])
        for step, value in enumerate(values, 1)
    ]


def coset_sum(values):
    while len(values) > 1:
        half = len(values) // 2
        values = [values[i] + values[i + half] for i in range(half)]
    return values[0]


def shards(latent_grad, features, head_weight):
    n_time, n_rows = lax.axis_size("tm"), lax.axis_size("rows")
    z = Sizes(n_time, n_rows, latent_grad.shape, features.shape)
    params = pltpu.CompilerParams(vmem_limit_bytes=32 * 1024 * 1024)
    f32, bf16 = jnp.float32, jnp.bfloat16
    hbm, vmem = pl.BlockSpec(memory_space=pltpu.HBM), pl.BlockSpec(memory_space=pltpu.VMEM)
    cells = z.grid_rows * z.width
    elements = cells * z.channels
    products = z.cols * z.grid_rows * LANES * z.channels
    flat = features.reshape(cells, z.channels)
    windows = pl.pallas_call(
        functools.partial(window_kernel, z),
        out_shape=[jax.ShapeDtypeStruct((z.all_frames * z.feat, LANES), bf16)] * n_rows,
        in_specs=[hbm],
        scratch_shapes=[pltpu.VMEM((z.feat, z.tokens), bf16), pltpu.SemaphoreType.DMA],
        compiler_params=params,
        name="band_windows",
    )(in_hbm(latent_grad.T))
    bands = [windows[0]] + rotate(windows[1:], "rows")
    sort, place = sort_rows(z), place_lanes(z)
    act, slope, sort, place = pl.pallas_call(
        functools.partial(prepare_kernel, z),
        out_shape=[
            jax.ShapeDtypeStruct((z.grid_rows * LANES, z.channels), bf16),
            jax.ShapeDtypeStruct((cells, z.channels), f32),
            jax.ShapeDtypeStruct(sort.shape, bf16),
            jax.ShapeDtypeStruct(place.shape, bf16),
        ],
        in_specs=[hbm] * 3,
        out_specs=[vmem] * 4,
        scratch_shapes=[pltpu.VMEM((cells, z.channels), bf16), pltpu.SemaphoreType.DMA((2 + z.frames,))],
        compiler_params=params,
        cost_estimate=pl.CostEstimate(
            flops=10 * elements, bytes_accessed=9 * elements, transcendentals=elements
        ),
        name="act_and_slope",
    )(in_hbm(flat), in_hbm(sort), in_hbm(place))
    parts = pl.pallas_call(
        functools.partial(frames_kernel, z),
        out_shape=[jax.ShapeDtypeStruct((n_rows, z.frames_x * z.feat, LANES), bf16)] * n_time,
        compiler_params=params,
        name="frame_windows",
    )(*bands)
    moved = [parts[0]] + exchange(parts[1:], "tm")
    pieces = pl.pallas_call(
        functools.partial(weight_kernel, z),
        out_shape=[
            jax.ShapeDtypeStruct((z.piece, z.channels), bf16 if s else f32) for s in range(n_time)
        ]
        + [jax.ShapeDtypeStruct((z.cols, z.grid_rows * LANES), bf16)],
        scratch_shapes=[
            pltpu.VMEM((n_rows * z.frames_x * z.feat, n_time * LANES), bf16),
            pltpu.VMEM((z.cols, z.channels), f32),
        ],
        compiler_params=params,
        cost_estimate=pl.CostEstimate(flops=2 * products, bytes_accessed=4 * elements, transcendentals=0),
        name="weight_term",
    )(*moved, sort, place, act)
    *pieces, cols = pieces
    grad = pl.pallas_call(
        functools.partial(features_kernel, z),
        out_shape=jax.ShapeDtypeStruct((cells, z.channels), bf16),
        compiler_params=params,
        cost_estimate=pl.CostEstimate(flops=2 * products, bytes_accessed=8 * elements, transcendentals=0),
        name="features_grad",
    )(cols, slope, head_weight)
    arrived = exchange(pieces[1:], "tm")
    mine = coset_sum([pieces[0]] + [value.astype(f32) for value in arrived]).astype(bf16)
    arrived = rotate([mine] * (n_rows - 1), "rows")
    whole = coset_sum([value.astype(f32) for value in [mine] + arrived])
    scale = 1.0 / math.sqrt(cells * n_time * n_rows)
    whole = (whole * scale).astype(bf16)
    arrived = exchange([whole] * (n_time - 1), "tm")
    weight_grad = pl.pallas_call(
        functools.partial(join_kernel, z),
        out_shape=jax.ShapeDtypeStruct((TAPS * z.latent, z.channels), f32),
        scratch_shapes=[pltpu.VMEM((z.cols, z.channels), f32)],
        compiler_params=params,
        name="join_pieces",
    )(whole, *arrived)
    return (grad.reshape(features.shape), weight_grad)


def solution(mesh):
    return jax.shard_map(
        shards,
        mesh=mesh,
        in_specs=(P(("dp", "tm"), "rows"), P(("dp", "tm"), "rows", None, None), P()),
        out_specs=(P(("dp", "tm"), "rows", None, None), P("dp", None)),
        check_vma=False,
    )
```

```python
import functools
import math

import jax
import jax.numpy as jnp
import numpy as np
from jax import lax
from jax.experimental import pallas as pl
from jax.experimental.pallas import tpu as pltpu
from jax.sharding import PartitionSpec as P

LANES = 128
TAPS = 27


class Sizes:
    def __init__(self, n_time, n_rows, latent_shape, features_shape):
        self.n_time, self.n_rows = n_time, n_rows
        self.frames, self.rows, self.width, self.channels = features_shape
        self.tokens, self.feat = latent_shape
        self.latent = self.feat * n_rows // 4
        self.cycle = 2 * n_time
        self.row_tokens = self.width // 2
        self.band = self.rows // 2
        self.band_x = self.band + 2
        self.frames_x = self.frames + 2
        self.all_frames = self.frames * n_time
        self.band_cycles = self.band * self.row_tokens // self.cycle
        self.halo_cycles = -(-self.row_tokens // self.cycle)
        self.halo = 2 * self.halo_cycles
        self.lanes = 2 * self.band_cycles + 2 * self.halo
        self.sources = n_time * n_rows
        self.grid_rows = self.frames * self.rows
        self.piece_taps = -(-TAPS // n_time)
        self.piece = self.piece_taps * self.latent
        self.cols = self.piece * n_time


def sort_rows(z):
    count = z.n_rows * z.frames_x * z.feat
    out = np.zeros((count, count), np.float32)
    part = z.feat // 4
    for r in range(z.n_rows):
        for t in range(z.frames_x):
            for e in range(part):
                for p in range(2):
                    for q in range(2):
                        source = (r * z.frames_x + t) * z.feat + 4 * e + 2 * p + q
                        target = ((q * 2 + p) * z.frames_x + t) * z.latent + r * part + e
                        out[target, source] = 1
    return jnp.asarray(out, jnp.bfloat16)


def place_lanes(z):
    out = np.zeros((2, z.n_time, LANES, z.band_x, LANES), np.float32)
    for q in range(2):
        for i in range(z.n_time):
            for lane in range(z.lanes):
                place = z.cycle - 1 - i if lane % 2 else i
                token = (lane // 2 - z.halo_cycles) * z.cycle + place + z.row_tokens
                if 0 <= token < z.band_x * z.row_tokens:
                    out[q, i, lane, token // z.row_tokens, 2 * (token % z.row_tokens) + q] = 1
    return jnp.asarray(out.reshape(2 * z.n_time * LANES, z.band_x * LANES), jnp.bfloat16)


def window_kernel(z, *refs):
    token_refs, out_refs = refs[: z.n_time], refs[z.n_time :]
    time, band = lax.axis_index("tm"), lax.axis_index("rows")
    lane = lax.broadcasted_iota(jnp.int32, (z.feat, LANES), 1)
    last = z.tokens // LANES - 2
    for step, out_ref in enumerate(out_refs):
        r = band ^ step
        low = jnp.where(r == 0, z.halo, 0)
        high = jnp.where(r == z.n_rows - 1, z.lanes - z.halo, z.lanes)
        inside = (lane >= low) & (lane < high)
        blocks = [[] for _ in token_refs]
        for t in range(z.frames_x):
            frame = time * z.frames + t
            start = 2 * (frame * z.n_rows + r) * z.band_cycles - z.halo
            tile = jnp.clip(start >> 7, 0, last)
            turn = (2 * LANES - (start - tile * LANES)) & (2 * LANES - 1)
            kept = inside & (frame < z.all_frames)
            for ref, held in zip(token_refs, blocks):
                value = ref[:, pl.ds(pl.multiple_of(tile * LANES, LANES), 2 * LANES)]
                value = pltpu.roll(value.astype(jnp.float32), turn, 1)[:, :LANES]
                held.append(jnp.where(kept, value, 0.0))
        for i, held in enumerate(blocks):
            out_ref[time ^ i] = jnp.concatenate(held, axis=0).astype(jnp.bfloat16)


def prepare_kernel(
    z, features_ref, sort_ref, place_ref, tokens_ref, act_ref, slope_ref, sort_out, place_out, tokens_out, held_ref, sems
):
    cells = z.rows * z.width
    frames = [slice(t * cells, (t + 1) * cells) for t in range(z.frames)]
    loads = [
        pltpu.make_async_copy(features_ref.at[here], held_ref.at[here], sems.at[3 + t])
        for t, here in enumerate(frames)
    ]
    copies = [
        pltpu.make_async_copy(sort_ref, sort_out, sems.at[0]),
        pltpu.make_async_copy(place_ref, place_out, sems.at[1]),
        pltpu.make_async_copy(tokens_ref, tokens_out, sems.at[2]),
    ]
    for copy in loads + copies:
        copy.start()
    for row in range(z.grid_rows):
        if row % z.rows == 0:
            loads[row // z.rows].wait()
        here = slice(row * z.width, (row + 1) * z.width)
        hidden = held_ref[here, :].astype(jnp.float32)
        sig = 0.5 + 0.5 * jnp.tanh(0.5 * hidden)
        act = hidden * sig
        act_ref[row * LANES : row * LANES + z.width, :] = act.astype(jnp.bfloat16)
        shape = (LANES - z.width, z.channels)
        act_ref[row * LANES + z.width : (row + 1) * LANES, :] = jnp.zeros(shape, jnp.bfloat16)
        slope_ref[here, :] = sig * (1.0 + hidden * (1.0 - sig))
    for copy in copies:
        copy.wait()


def slot_start(z, piece):
    return pl.multiple_of((lax.axis_index("tm") ^ piece) * z.piece, z.piece)


def last_first(count):
    return [count - 1, *range(1, count - 1)]


def fill_cols(z, moved_refs, sort_ref, place_ref, cols_ref, held_ref):
    count = z.frames_x * z.feat
    rows = z.n_rows * count
    band = lax.axis_index("rows")
    for step, ref in zip([0] + last_first(z.n_rows), moved_refs):
        start = pl.multiple_of((band ^ step) * count, count)
        for i in range(z.n_time):
            held_ref[pl.ds(start, count), i * LANES : (i + 1) * LANES] = ref[i]
    ordered = jnp.dot(
        sort_ref[...], held_ref[...], preferred_element_type=jnp.float32
    ).astype(jnp.bfloat16)
    half = rows // 2
    pair = jnp.concatenate([ordered[:half], ordered[half:]], axis=1)
    grid = jnp.dot(pair, place_ref[...], preferred_element_type=jnp.float32)
    slots = [slot_start(z, piece) for piece in range(z.n_time)]

    def tap_rows(tap):
        start = slots[tap // z.piece_taps] + tap % z.piece_taps * z.latent
        return pl.ds(pl.multiple_of(start, z.latent), z.latent)

    for a in range(z.band_x):
        block = grid[:, a * LANES : (a + 1) * LANES]
        for kw in range(3):
            turned = block if kw == 1 else pltpu.roll(block, LANES - 1 if kw == 0 else 1, 1)
            turned = turned.astype(jnp.bfloat16)
            for p in range(2):
                for t in range(z.frames_x):
                    at = (p * z.frames_x + t) * z.latent
                    value = turned[at : at + z.latent]
                    for kt in range(3):
                        for kh in range(3):
                            frame, row = t - 2 + kt, 2 * (a - 1) + p - 1 + kh
                            if 0 <= frame < z.frames and 0 <= row < z.rows:
                                tap = (kt * 3 + kh) * 3 + kw
                                lane = (frame * z.rows + row) * LANES
                                cols_ref[tap_rows(tap), lane : lane + LANES] = value
    for tap in range(TAPS, z.n_time * z.piece_taps):
        cols_ref[tap_rows(tap), :] = jnp.zeros((z.latent, z.grid_rows * LANES), jnp.bfloat16)


def weight_kernel(z, *refs):
    moved_refs, (sort_ref, place_ref, act_ref) = refs[: z.n_rows], refs[z.n_rows : z.n_rows + 3]
    out_refs, cols_ref, held_ref = refs[z.n_rows + 3 : -2], refs[-2], refs[-1]
    fill_cols(z, moved_refs, sort_ref, place_ref, cols_ref, held_ref)
    total = jnp.dot(cols_ref[z.piece :, :], act_ref[...], preferred_element_type=jnp.float32)
    for step, ref in enumerate(out_refs):
        ref[...] = total[step * z.piece : (step + 1) * z.piece].astype(jnp.bfloat16)


def own_kernel(z, cols_ref, act_ref, out_ref):
    out_ref[...] = jnp.dot(cols_ref[: z.piece, :], act_ref[...], preferred_element_type=jnp.float32)


def features_kernel(z, cols_ref, slope_ref, weight_ref, out_ref, held_ref):
    for piece in range(z.n_time):
        first = piece * z.piece
        count = max(0, min(z.piece, TAPS * z.latent - first))
        start = slot_start(z, piece)
        if count:
            held_ref[pl.ds(start, count), :] = weight_ref[first : first + count, :]
        if count < z.piece:
            start = pl.multiple_of(start + count, z.latent)
            held_ref[pl.ds(start, z.piece - count), :] = jnp.zeros((z.piece - count, z.channels), jnp.bfloat16)
    step = 4
    for first in range(0, z.grid_rows, step):
        count = min(step, z.grid_rows - first)
        part = cols_ref[:, first * LANES : (first + count) * LANES]
        product = lax.dot_general(
            part, held_ref[...], (((0,), (0,)), ((), ())), preferred_element_type=jnp.float32
        )
        for k in range(count):
            here = slice((first + k) * z.width, (first + k + 1) * z.width)
            value = product[k * LANES : k * LANES + z.width] * slope_ref[here, :]
            out_ref[here, :] = value.astype(jnp.bfloat16)


def join_kernel(z, *refs):
    piece_refs, (out_ref, held_ref, sems) = refs[: z.n_time], refs[z.n_time :]
    me = lax.axis_index("tm")
    whole, tail = divmod(TAPS * z.latent, z.piece)

    def each(act):
        for step in range(z.n_time):
            place = me ^ step
            start = pl.multiple_of(place * z.piece, z.piece)

            def copy(count):
                source = held_ref.at[step, pl.ds(0, count)]
                act(pltpu.make_async_copy(source, out_ref.at[pl.ds(start, count)], sems.at[step]))

            pl.when(place < whole)(functools.partial(copy, z.piece))
            if tail:
                pl.when(place == whole)(functools.partial(copy, tail))

    for step, ref in enumerate(piece_refs):
        held_ref[step] = ref[...].astype(jnp.float32)
    each(lambda copy: copy.start())
    each(lambda copy: copy.wait())


def in_hbm(value):
    return pltpu.with_memory_space_constraint(value, pltpu.HBM)


def exchange(values, axis):
    size = lax.axis_size(axis)
    return [
        lax.ppermute(value, axis, [(i, i ^ step) for i in range(size)])
        for step, value in enumerate(values, 1)
    ]


def coset_sum(values):
    while len(values) > 1:
        half = len(values) // 2
        values = [values[i] + values[i + half] for i in range(half)]
    return values[0]


def shards(latent_grad, features, head_weight):
    n_time, n_rows = lax.axis_size("tm"), lax.axis_size("rows")
    z = Sizes(n_time, n_rows, latent_grad.shape, features.shape)
    params = pltpu.CompilerParams(vmem_limit_bytes=32 * 1024 * 1024)
    f32, bf16 = jnp.float32, jnp.bfloat16
    hbm, vmem = pl.BlockSpec(memory_space=pltpu.HBM), pl.BlockSpec(memory_space=pltpu.VMEM)
    cells = z.grid_rows * z.width
    elements = cells * z.channels
    products = z.cols * z.grid_rows * LANES * z.channels
    flat = features.reshape(cells, z.channels)
    tokens = latent_grad.T
    arrived = exchange([tokens] * (n_time - 1), "tm")
    sort, place = sort_rows(z), place_lanes(z)
    act, slope, sort, place, tokens = pl.pallas_call(
        functools.partial(prepare_kernel, z),
        out_shape=[
            jax.ShapeDtypeStruct((z.grid_rows * LANES, z.channels), bf16),
            jax.ShapeDtypeStruct((cells, z.channels), f32),
            jax.ShapeDtypeStruct(sort.shape, bf16),
            jax.ShapeDtypeStruct(place.shape, bf16),
            jax.ShapeDtypeStruct(tokens.shape, bf16),
        ],
        in_specs=[hbm] * 4,
        out_specs=[vmem] * 5,
        scratch_shapes=[pltpu.VMEM((cells, z.channels), bf16), pltpu.SemaphoreType.DMA((3 + z.frames,))],
        compiler_params=params,
        cost_estimate=pl.CostEstimate(
            flops=10 * elements, bytes_accessed=9 * elements, transcendentals=elements
        ),
        name="act_and_slope",
    )(in_hbm(flat), in_hbm(sort), in_hbm(place), in_hbm(tokens))
    windows = pl.pallas_call(
        functools.partial(window_kernel, z),
        out_shape=[jax.ShapeDtypeStruct((n_time, z.frames_x * z.feat, LANES), bf16)] * n_rows,
        compiler_params=params,
        name="latent_windows",
    )(tokens, *arrived)
    arrived = exchange(windows[1:], "rows")
    moved = [windows[0]] + [arrived[step - 1] for step in last_first(n_rows)]
    *pieces, cols = pl.pallas_call(
        functools.partial(weight_kernel, z),
        out_shape=[jax.ShapeDtypeStruct((z.piece, z.channels), bf16)] * (n_time - 1)
        + [jax.ShapeDtypeStruct((z.cols, z.grid_rows * LANES), bf16)],
        scratch_shapes=[pltpu.VMEM((n_rows * z.frames_x * z.feat, n_time * LANES), bf16)],
        compiler_params=params,
        cost_estimate=pl.CostEstimate(flops=2 * products, bytes_accessed=4 * elements, transcendentals=0),
        name="weight_term",
    )(*moved, sort, place, act)
    arrived = exchange(pieces, "tm")
    own = pl.pallas_call(
        functools.partial(own_kernel, z),
        out_shape=jax.ShapeDtypeStruct((z.piece, z.channels), f32),
        compiler_params=params,
        cost_estimate=pl.CostEstimate(
            flops=2 * products // n_time, bytes_accessed=2 * elements, transcendentals=0
        ),
        name="own_piece",
    )(cols, act)
    for step in last_first(n_time):
        own = own + arrived[step - 1].astype(f32)
    mine = own.astype(bf16)
    cols, mine = lax.optimization_barrier((cols, mine))
    grad = pl.pallas_call(
        functools.partial(features_kernel, z),
        out_shape=jax.ShapeDtypeStruct((cells, z.channels), bf16),
        scratch_shapes=[pltpu.VMEM((z.cols, z.channels), bf16)],
        compiler_params=params,
        cost_estimate=pl.CostEstimate(flops=2 * products, bytes_accessed=8 * elements, transcendentals=0),
        name="features_grad",
    )(cols, slope, head_weight)
    arrived = exchange([mine] * (n_rows - 1), "rows")
    whole = coset_sum([value.astype(f32) for value in [mine] + arrived])
    scale = 1.0 / math.sqrt(cells * n_time * n_rows)
    whole = (whole * scale).astype(bf16)
    whole, grad = lax.optimization_barrier((whole, grad))
    pieces = [whole] + exchange([whole] * (n_time - 1), "tm")
    weight_grad = pl.pallas_call(
        functools.partial(join_kernel, z),
        out_shape=jax.ShapeDtypeStruct((TAPS * z.latent, z.channels), f32),
        in_specs=[vmem] * n_time,
        out_specs=hbm,
        scratch_shapes=[
            pltpu.VMEM((n_time, z.piece, z.channels), f32),
            pltpu.SemaphoreType.DMA((n_time,)),
        ],
        compiler_params=params,
        name="join_pieces",
    )(*pieces)
    return (grad.reshape(features.shape), weight_grad)


def solution(mesh):
    return jax.shard_map(
        shards,
        mesh=mesh,
        in_specs=(P(("dp", "tm"), "rows"), P(("dp", "tm"), "rows", None, None), P()),
        out_specs=(P(("dp", "tm"), "rows", None, None), P("dp", None)),
        check_vma=False,
    )
```

```python
import functools
import math

import jax
import jax.numpy as jnp
import numpy as np
from jax import lax
from jax.experimental import pallas as pl
from jax.experimental.pallas import tpu as pltpu
from jax.sharding import PartitionSpec as P

LANES = 128
TAPS = 27


class Sizes:
    def __init__(self, n_time, n_rows, latent_shape, features_shape):
        self.n_time, self.n_rows = n_time, n_rows
        self.frames, self.rows, self.width, self.channels = features_shape
        self.tokens, self.feat = latent_shape
        self.latent = self.feat * n_rows // 4
        self.cycle = 2 * n_time
        self.row_tokens = self.width // 2
        self.band = self.rows // 2
        self.band_x = self.band + 2
        self.frames_x = self.frames + 2
        self.all_frames = self.frames * n_time
        self.band_cycles = self.band * self.row_tokens // self.cycle
        self.halo_cycles = -(-self.row_tokens // self.cycle)
        self.halo = 2 * self.halo_cycles
        self.lanes = 2 * self.band_cycles + 2 * self.halo
        self.sources = n_time * n_rows
        self.grid_rows = self.frames * self.rows
        self.piece_taps = -(-TAPS // n_time)
        self.piece = self.piece_taps * self.latent
        self.cols = self.piece * n_time


def sort_rows(z):
    count = z.n_rows * z.frames_x * z.feat
    out = np.zeros((count, count), np.float32)
    part = z.feat // 4
    for r in range(z.n_rows):
        for t in range(z.frames_x):
            for e in range(part):
                for p in range(2):
                    for q in range(2):
                        source = (r * z.frames_x + t) * z.feat + 4 * e + 2 * p + q
                        target = ((q * 2 + p) * z.frames_x + t) * z.latent + r * part + e
                        out[target, source] = 1
    return jnp.asarray(out, jnp.bfloat16)


def place_lanes(z):
    out = np.zeros((2, z.n_time, LANES, z.band_x, LANES), np.float32)
    for q in range(2):
        for i in range(z.n_time):
            for lane in range(z.lanes):
                place = z.cycle - 1 - i if lane % 2 else i
                token = (lane // 2 - z.halo_cycles) * z.cycle + place + z.row_tokens
                if 0 <= token < z.band_x * z.row_tokens:
                    out[q, i, lane, token // z.row_tokens, 2 * (token % z.row_tokens) + q] = 1
    return jnp.asarray(out.reshape(2 * z.n_time * LANES, z.band_x * LANES), jnp.bfloat16)


def window_kernel(z, *refs):
    token_refs, out_refs = refs[: z.n_time], refs[z.n_time :]
    time, band = lax.axis_index("tm"), lax.axis_index("rows")
    lane = lax.broadcasted_iota(jnp.int32, (z.feat, LANES), 1)
    last = z.tokens // LANES - 2
    for step, out_ref in enumerate(out_refs):
        r = band ^ step
        low = jnp.where(r == 0, z.halo, 0)
        high = jnp.where(r == z.n_rows - 1, z.lanes - z.halo, z.lanes)
        inside = (lane >= low) & (lane < high)
        blocks = [[] for _ in token_refs]
        for t in range(z.frames_x):
            frame = time * z.frames + t
            start = 2 * (frame * z.n_rows + r) * z.band_cycles - z.halo
            tile = jnp.clip(start >> 7, 0, last)
            turn = (2 * LANES - (start - tile * LANES)) & (2 * LANES - 1)
            kept = inside & (frame < z.all_frames)
            for ref, held in zip(token_refs, blocks):
                value = ref[:, pl.ds(pl.multiple_of(tile * LANES, LANES), 2 * LANES)]
                value = pltpu.roll(value.astype(jnp.float32), turn, 1)[:, :LANES]
                held.append(jnp.where(kept, value, 0.0))
        for i, held in enumerate(blocks):
            out_ref[time ^ i] = jnp.concatenate(held, axis=0).astype(jnp.bfloat16)


def prepare_kernel(
    z, features_ref, sort_ref, place_ref, tokens_ref, act_ref, slope_ref, sort_out, place_out, tokens_out, held_ref, sems
):
    cells = z.rows * z.width
    frames = [slice(t * cells, (t + 1) * cells) for t in range(z.frames)]
    loads = [
        pltpu.make_async_copy(features_ref.at[here], held_ref.at[here], sems.at[3 + t])
        for t, here in enumerate(frames)
    ]
    copies = [
        pltpu.make_async_copy(sort_ref, sort_out, sems.at[0]),
        pltpu.make_async_copy(place_ref, place_out, sems.at[1]),
        pltpu.make_async_copy(tokens_ref, tokens_out, sems.at[2]),
    ]
    for copy in loads + copies:
        copy.start()
    for row in range(z.grid_rows):
        if row % z.rows == 0:
            loads[row // z.rows].wait()
        here = slice(row * z.width, (row + 1) * z.width)
        hidden = held_ref[here, :].astype(jnp.float32)
        sig = 0.5 + 0.5 * jnp.tanh(0.5 * hidden)
        act = hidden * sig
        act_ref[row * LANES : row * LANES + z.width, :] = act.astype(jnp.bfloat16)
        shape = (LANES - z.width, z.channels)
        act_ref[row * LANES + z.width : (row + 1) * LANES, :] = jnp.zeros(shape, jnp.bfloat16)
        slope_ref[here, :] = sig * (1.0 + hidden * (1.0 - sig))
    for copy in copies:
        copy.wait()


def slot_start(z, piece):
    return pl.multiple_of((lax.axis_index("tm") ^ piece) * z.piece, z.piece)


def last_first(count):
    return [count - 1, *range(1, count - 1)]


def turned_grid(z, moved_refs, sort_ref, place_ref, held_ref):
    count = z.frames_x * z.feat
    rows = z.n_rows * count
    band = lax.axis_index("rows")
    for step, ref in zip([0] + last_first(z.n_rows), moved_refs):
        start = pl.multiple_of((band ^ step) * count, count)
        for i in range(z.n_time):
            held_ref[pl.ds(start, count), i * LANES : (i + 1) * LANES] = ref[i]
    ordered = jnp.dot(
        sort_ref[...], held_ref[...], preferred_element_type=jnp.float32
    ).astype(jnp.bfloat16)
    half = rows // 2
    pair = jnp.concatenate([ordered[:half], ordered[half:]], axis=1)
    grid = jnp.dot(pair, place_ref[...], preferred_element_type=jnp.float32)
    turned = {}
    for a in range(z.band_x):
        block = grid[:, a * LANES : (a + 1) * LANES]
        for kw, turn in enumerate((LANES - 1, 0, 1)):
            value = pltpu.roll(block, turn, 1) if turn else block
            turned[a, kw] = value.astype(jnp.bfloat16)
    return turned


def fill_cols(z, turned, frame, cols_ref):
    for tap in range(z.n_time * z.piece_taps):
        start = slot_start(z, tap // z.piece_taps) + tap % z.piece_taps * z.latent
        here = pl.ds(pl.multiple_of(start, z.latent), z.latent)
        if tap >= TAPS:
            cols_ref[here, :] = jnp.zeros((z.latent, z.rows * LANES), jnp.bfloat16)
            continue
        kt, kh, kw = tap // 9, tap // 3 % 3, tap % 3
        t = frame + 2 - kt
        for row in range(z.rows):
            a, p = divmod(row + 1 - kh + 2, 2)
            at = (p * z.frames_x + t) * z.latent
            cols_ref[here, row * LANES : (row + 1) * LANES] = turned[a, kw][at : at + z.latent]


def weight_kernel(z, *refs):
    moved_refs, (sort_ref, place_ref, act_ref) = refs[: z.n_rows], refs[z.n_rows : z.n_rows + 3]
    out_refs, cols_refs, held_ref = refs[z.n_rows + 3 : -1 - z.frames], refs[-1 - z.frames : -1], refs[-1]
    turned = turned_grid(z, moved_refs, sort_ref, place_ref, held_ref)
    total = 0.0
    for frame, cols_ref in enumerate(cols_refs):
        fill_cols(z, turned, frame, cols_ref)
        act = act_ref[frame * z.rows * LANES : (frame + 1) * z.rows * LANES, :]
        total = total + jnp.dot(cols_ref[z.piece :, :], act, preferred_element_type=jnp.float32)
    for step, ref in enumerate(out_refs):
        ref[...] = total[step * z.piece : (step + 1) * z.piece].astype(jnp.bfloat16)


def own_kernel(z, *refs):
    cols_refs, (act_ref, out_ref) = refs[: z.frames], refs[z.frames :]
    total = 0.0
    for frame, cols_ref in enumerate(cols_refs):
        act = act_ref[frame * z.rows * LANES : (frame + 1) * z.rows * LANES, :]
        total = total + jnp.dot(cols_ref[: z.piece, :], act, preferred_element_type=jnp.float32)
    out_ref[...] = total


def features_kernel(z, *refs):
    cols_refs, (slope_ref, weight_ref, out_ref, held_ref) = refs[: z.frames], refs[z.frames :]
    for piece in range(z.n_time):
        first = piece * z.piece
        count = max(0, min(z.piece, TAPS * z.latent - first))
        start = slot_start(z, piece)
        if count:
            held_ref[pl.ds(start, count), :] = weight_ref[first : first + count, :]
        if count < z.piece:
            start = pl.multiple_of(start + count, z.latent)
            held_ref[pl.ds(start, z.piece - count), :] = jnp.zeros((z.piece - count, z.channels), jnp.bfloat16)
    step = 4
    for frame, cols_ref in enumerate(cols_refs):
        for first in range(0, z.rows, step):
            count = min(step, z.rows - first)
            part = cols_ref[:, first * LANES : (first + count) * LANES]
            product = lax.dot_general(
                part, held_ref[...], (((0,), (0,)), ((), ())), preferred_element_type=jnp.float32
            )
            for k in range(count):
                row = frame * z.rows + first + k
                here = slice(row * z.width, (row + 1) * z.width)
                value = product[k * LANES : k * LANES + z.width] * slope_ref[here, :]
                out_ref[here, :] = value.astype(jnp.bfloat16)


def join_kernel(z, *refs):
    piece_refs, (out_ref, held_ref, sems) = refs[: z.n_time], refs[z.n_time :]
    me = lax.axis_index("tm")
    whole, tail = divmod(TAPS * z.latent, z.piece)

    def each(step, act):
        place = me ^ step
        start = pl.multiple_of(place * z.piece, z.piece)

        def copy(count):
            source = held_ref.at[step, pl.ds(0, count)]
            act(pltpu.make_async_copy(source, out_ref.at[pl.ds(start, count)], sems.at[step]))

        pl.when(place < whole)(functools.partial(copy, z.piece))
        if tail:
            pl.when(place == whole)(functools.partial(copy, tail))

    for step, ref in enumerate(piece_refs):
        held_ref[step] = ref[...].astype(jnp.float32)
        each(step, lambda copy: copy.start())
    for step in range(z.n_time):
        each(step, lambda copy: copy.wait())


def in_hbm(value):
    return pltpu.with_memory_space_constraint(value, pltpu.HBM)


def exchange(values, axis):
    size = lax.axis_size(axis)
    return [
        lax.ppermute(value, axis, [(i, i ^ step) for i in range(size)])
        for step, value in enumerate(values, 1)
    ]


def coset_sum(values):
    while len(values) > 1:
        half = len(values) // 2
        values = [values[i] + values[i + half] for i in range(half)]
    return values[0]


def shards(latent_grad, features, head_weight):
    n_time, n_rows = lax.axis_size("tm"), lax.axis_size("rows")
    z = Sizes(n_time, n_rows, latent_grad.shape, features.shape)
    params = pltpu.CompilerParams(vmem_limit_bytes=32 * 1024 * 1024)
    f32, bf16 = jnp.float32, jnp.bfloat16
    hbm, vmem = pl.BlockSpec(memory_space=pltpu.HBM), pl.BlockSpec(memory_space=pltpu.VMEM)
    cells = z.grid_rows * z.width
    elements = cells * z.channels
    products = z.cols * z.grid_rows * LANES * z.channels
    flat = features.reshape(cells, z.channels)
    tokens = latent_grad.T
    arrived = exchange([tokens] * (n_time - 1), "tm")
    sort, place = sort_rows(z), place_lanes(z)
    act, slope, sort, place, tokens = pl.pallas_call(
        functools.partial(prepare_kernel, z),
        out_shape=[
            jax.ShapeDtypeStruct((z.grid_rows * LANES, z.channels), bf16),
            jax.ShapeDtypeStruct((cells, z.channels), f32),
            jax.ShapeDtypeStruct(sort.shape, bf16),
            jax.ShapeDtypeStruct(place.shape, bf16),
            jax.ShapeDtypeStruct(tokens.shape, bf16),
        ],
        in_specs=[hbm] * 4,
        out_specs=[vmem] * 5,
        scratch_shapes=[pltpu.VMEM((cells, z.channels), bf16), pltpu.SemaphoreType.DMA((3 + z.frames,))],
        compiler_params=params,
        cost_estimate=pl.CostEstimate(
            flops=10 * elements, bytes_accessed=9 * elements, transcendentals=elements
        ),
        name="act_and_slope",
    )(in_hbm(flat), in_hbm(sort), in_hbm(place), in_hbm(tokens))
    windows = pl.pallas_call(
        functools.partial(window_kernel, z),
        out_shape=[jax.ShapeDtypeStruct((n_time, z.frames_x * z.feat, LANES), bf16)] * n_rows,
        compiler_params=params,
        name="latent_windows",
    )(tokens, *arrived)
    arrived = exchange(windows[1:], "rows")
    moved = [windows[0]] + [arrived[step - 1] for step in last_first(n_rows)]
    outs = pl.pallas_call(
        functools.partial(weight_kernel, z),
        out_shape=[jax.ShapeDtypeStruct((z.piece, z.channels), bf16)] * (n_time - 1)
        + [jax.ShapeDtypeStruct((z.cols, z.rows * LANES), bf16)] * z.frames,
        scratch_shapes=[pltpu.VMEM((n_rows * z.frames_x * z.feat, n_time * LANES), bf16)],
        compiler_params=params,
        cost_estimate=pl.CostEstimate(flops=2 * products, bytes_accessed=4 * elements, transcendentals=0),
        name="weight_term",
    )(*moved, sort, place, act)
    pieces, cols = outs[: n_time - 1], outs[n_time - 1 :]
    arrived = exchange(pieces, "tm")
    own = pl.pallas_call(
        functools.partial(own_kernel, z),
        out_shape=jax.ShapeDtypeStruct((z.piece, z.channels), f32),
        compiler_params=params,
        cost_estimate=pl.CostEstimate(
            flops=2 * products // n_time, bytes_accessed=2 * elements, transcendentals=0
        ),
        name="own_piece",
    )(*cols, act)
    for step in last_first(n_time):
        own = own + arrived[step - 1].astype(f32)
    mine = own.astype(bf16)
    cols, mine = lax.optimization_barrier((cols, mine))
    grad = pl.pallas_call(
        functools.partial(features_kernel, z),
        out_shape=jax.ShapeDtypeStruct((cells, z.channels), bf16),
        scratch_shapes=[pltpu.VMEM((z.cols, z.channels), bf16)],
        compiler_params=params,
        cost_estimate=pl.CostEstimate(flops=2 * products, bytes_accessed=8 * elements, transcendentals=0),
        name="features_grad",
    )(*cols, slope, head_weight)
    arrived = exchange([mine] * (n_rows - 1), "rows")
    whole = coset_sum([value.astype(f32) for value in [mine] + arrived])
    scale = 1.0 / math.sqrt(cells * n_time * n_rows)
    whole = (whole * scale).astype(bf16)
    whole, grad = lax.optimization_barrier((whole, grad))
    pieces = [whole] + exchange([whole] * (n_time - 1), "tm")
    weight_grad = pl.pallas_call(
        functools.partial(join_kernel, z),
        out_shape=jax.ShapeDtypeStruct((TAPS * z.latent, z.channels), f32),
        in_specs=[vmem] * n_time,
        out_specs=hbm,
        scratch_shapes=[
            pltpu.VMEM((n_time, z.piece, z.channels), f32),
            pltpu.SemaphoreType.DMA((n_time,)),
        ],
        compiler_params=params,
        name="join_pieces",
    )(*pieces)
    return (grad.reshape(features.shape), weight_grad)


def solution(mesh):
    return jax.shard_map(
        shards,
        mesh=mesh,
        in_specs=(P(("dp", "tm"), "rows"), P(("dp", "tm"), "rows", None, None), P()),
        out_specs=(P(("dp", "tm"), "rows", None, None), P("dp", None)),
        check_vma=False,
    )
```

```python
import functools
import math

import jax
import jax.numpy as jnp
import numpy as np
from jax import lax
from jax.experimental import pallas as pl
from jax.experimental.pallas import tpu as pltpu
from jax.sharding import PartitionSpec as P

LANES = 128
TAPS = 27


class Sizes:
    def __init__(self, n_time, n_rows, latent_shape, features_shape):
        self.n_time, self.n_rows = n_time, n_rows
        self.frames, self.rows, self.width, self.channels = features_shape
        self.tokens, self.feat = latent_shape
        self.latent = self.feat * n_rows // 4
        self.cycle = 2 * n_time
        self.row_tokens = self.width // 2
        self.band = self.rows // 2
        self.band_x = self.band + 2
        self.frames_x = self.frames + 2
        self.all_frames = self.frames * n_time
        self.band_cycles = self.band * self.row_tokens // self.cycle
        self.halo_cycles = -(-self.row_tokens // self.cycle)
        self.halo = 2 * self.halo_cycles
        self.lanes = 2 * self.band_cycles + 2 * self.halo
        self.sources = n_time * n_rows
        self.grid_rows = self.frames * self.rows
        self.piece_taps = -(-TAPS // n_time)
        self.piece = self.piece_taps * self.latent
        self.cols = self.piece * n_time


def sort_rows(z):
    count = z.n_rows * z.frames_x * z.feat
    out = np.zeros((count, count), np.float32)
    part = z.feat // 4
    for r in range(z.n_rows):
        for t in range(z.frames_x):
            for e in range(part):
                for p in range(2):
                    for q in range(2):
                        source = (r * z.frames_x + t) * z.feat + 4 * e + 2 * p + q
                        target = ((q * 2 + p) * z.frames_x + t) * z.latent + r * part + e
                        out[target, source] = 1
    return jnp.asarray(out, jnp.bfloat16)


def place_lanes(z):
    out = np.zeros((2, z.n_time, LANES, z.band_x, LANES), np.float32)
    for q in range(2):
        for i in range(z.n_time):
            for lane in range(z.lanes):
                place = z.cycle - 1 - i if lane % 2 else i
                token = (lane // 2 - z.halo_cycles) * z.cycle + place + z.row_tokens
                if 0 <= token < z.band_x * z.row_tokens:
                    out[q, i, lane, token // z.row_tokens, 2 * (token % z.row_tokens) + q] = 1
    return jnp.asarray(out.reshape(2 * z.n_time * LANES, z.band_x * LANES), jnp.bfloat16)


def window_kernel(z, *refs):
    token_refs, out_refs = refs[: z.n_time], refs[z.n_time :]
    time, band = lax.axis_index("tm"), lax.axis_index("rows")
    lane = lax.broadcasted_iota(jnp.int32, (z.feat, LANES), 1)
    last = z.tokens // LANES - 2
    for step, out_ref in enumerate(out_refs):
        r = band ^ step
        low = jnp.where(r == 0, z.halo, 0)
        high = jnp.where(r == z.n_rows - 1, z.lanes - z.halo, z.lanes)
        inside = (lane >= low) & (lane < high)
        blocks = [[] for _ in token_refs]
        for t in range(z.frames_x):
            frame = time * z.frames + t
            start = 2 * (frame * z.n_rows + r) * z.band_cycles - z.halo
            tile = jnp.clip(start >> 7, 0, last)
            turn = (2 * LANES - (start - tile * LANES)) & (2 * LANES - 1)
            kept = inside & (frame < z.all_frames)
            for ref, held in zip(token_refs, blocks):
                value = ref[:, pl.ds(pl.multiple_of(tile * LANES, LANES), 2 * LANES)]
                value = pltpu.roll(value.astype(jnp.float32), turn, 1)[:, :LANES]
                held.append(jnp.where(kept, value, 0.0))
        for i, held in enumerate(blocks):
            out_ref[time ^ i] = jnp.concatenate(held, axis=0).astype(jnp.bfloat16)


def prepare_kernel(
    z, features_ref, sort_ref, place_ref, tokens_ref, act_ref, slope_ref, sort_out, place_out, tokens_out, held_ref, sems
):
    cells = z.rows * z.width
    frames = [slice(t * cells, (t + 1) * cells) for t in range(z.frames)]
    loads = [
        pltpu.make_async_copy(features_ref.at[here], held_ref.at[here], sems.at[3 + t])
        for t, here in enumerate(frames)
    ]
    copies = [
        pltpu.make_async_copy(sort_ref, sort_out, sems.at[0]),
        pltpu.make_async_copy(place_ref, place_out, sems.at[1]),
        pltpu.make_async_copy(tokens_ref, tokens_out, sems.at[2]),
    ]
    for copy in loads + copies:
        copy.start()
    for row in range(z.grid_rows):
        if row % z.rows == 0:
            loads[row // z.rows].wait()
        here = slice(row * z.width, (row + 1) * z.width)
        hidden = held_ref[here, :].astype(jnp.float32)
        sig = 0.5 + 0.5 * jnp.tanh(0.5 * hidden)
        act = hidden * sig
        act_ref[row * LANES : row * LANES + z.width, :] = act.astype(jnp.bfloat16)
        shape = (LANES - z.width, z.channels)
        act_ref[row * LANES + z.width : (row + 1) * LANES, :] = jnp.zeros(shape, jnp.bfloat16)
        slope_ref[here, :] = sig * (1.0 + hidden * (1.0 - sig))
    for copy in copies:
        copy.wait()


def slot_start(z, piece):
    return pl.multiple_of((lax.axis_index("tm") ^ piece) * z.piece, z.piece)


def last_first(count):
    return [count - 1, *range(1, count - 1)]


def turned_grid(z, moved_refs, sort_ref, place_ref, held_ref):
    count = z.frames_x * z.feat
    rows = z.n_rows * count
    band = lax.axis_index("rows")
    for step, ref in zip([0] + last_first(z.n_rows), moved_refs):
        start = pl.multiple_of((band ^ step) * count, count)
        for i in range(z.n_time):
            held_ref[pl.ds(start, count), i * LANES : (i + 1) * LANES] = ref[i]
    ordered = jnp.dot(
        sort_ref[...], held_ref[...], preferred_element_type=jnp.float32
    ).astype(jnp.bfloat16)
    half = rows // 2
    pair = jnp.concatenate([ordered[:half], ordered[half:]], axis=1)
    grid = jnp.dot(pair, place_ref[...], preferred_element_type=jnp.float32)
    turned = {}
    for a in range(z.band_x):
        block = grid[:, a * LANES : (a + 1) * LANES]
        for kw, turn in enumerate((LANES - 1, 0, 1)):
            value = pltpu.roll(block, turn, 1) if turn else block
            turned[a, kw] = value.astype(jnp.bfloat16)
    return turned


def fill_cols(z, turned, frame, cols_ref, me=None):
    for tap in range(z.n_time * z.piece_taps):
        if me is None:
            start = slot_start(z, tap // z.piece_taps) + tap % z.piece_taps * z.latent
            here = pl.ds(pl.multiple_of(start, z.latent), z.latent)
        else:
            start = (tap // z.piece_taps ^ me) * z.piece + tap % z.piece_taps * z.latent
            here = slice(start, start + z.latent)
        if tap >= TAPS:
            cols_ref[here, :] = jnp.zeros((z.latent, z.rows * LANES), jnp.bfloat16)
            continue
        kt, kh, kw = tap // 9, tap // 3 % 3, tap % 3
        t = frame + 2 - kt
        for row in range(z.rows):
            a, p = divmod(row + 1 - kh + 2, 2)
            at = (p * z.frames_x + t) * z.latent
            cols_ref[here, row * LANES : (row + 1) * LANES] = turned[a, kw][at : at + z.latent]


def weight_kernel(z, *refs):
    moved_refs, (sort_ref, place_ref, act_ref) = refs[: z.n_rows], refs[z.n_rows : z.n_rows + 3]
    out_refs, cols_refs, held_ref = refs[z.n_rows + 3 : -1 - z.frames], refs[-1 - z.frames : -1], refs[-1]

    def term(me=None):
        turned = turned_grid(z, moved_refs, sort_ref, place_ref, held_ref)
        total = 0.0
        for frame, cols_ref in enumerate(cols_refs):
            fill_cols(z, turned, frame, cols_ref, me)
            act = act_ref[frame * z.rows * LANES : (frame + 1) * z.rows * LANES, :]
            total = total + jnp.dot(cols_ref[z.piece :, :], act, preferred_element_type=jnp.float32)
        for step, ref in enumerate(out_refs):
            ref[...] = total[step * z.piece : (step + 1) * z.piece].astype(jnp.bfloat16)

    if z.n_time > 4:
        term()
        return
    for me in range(z.n_time):
        pl.when(lax.axis_index("tm") == me)(functools.partial(term, me))


def own_kernel(z, *refs):
    cols_refs, (act_ref, out_ref) = refs[: z.frames], refs[z.frames :]
    total = 0.0
    for frame, cols_ref in enumerate(cols_refs):
        act = act_ref[frame * z.rows * LANES : (frame + 1) * z.rows * LANES, :]
        total = total + jnp.dot(cols_ref[: z.piece, :], act, preferred_element_type=jnp.float32)
    out_ref[...] = total


def features_kernel(z, *refs):
    cols_refs, (slope_ref, weight_ref, out_ref, held_ref) = refs[: z.frames], refs[z.frames :]
    for piece in range(z.n_time):
        first = piece * z.piece
        count = max(0, min(z.piece, TAPS * z.latent - first))
        start = slot_start(z, piece)
        if count:
            held_ref[pl.ds(start, count), :] = weight_ref[first : first + count, :]
        if count < z.piece:
            start = pl.multiple_of(start + count, z.latent)
            held_ref[pl.ds(start, z.piece - count), :] = jnp.zeros((z.piece - count, z.channels), jnp.bfloat16)
    step = 4
    for frame, cols_ref in enumerate(cols_refs):
        for first in range(0, z.rows, step):
            count = min(step, z.rows - first)
            part = cols_ref[:, first * LANES : (first + count) * LANES]
            product = lax.dot_general(
                part, held_ref[...], (((0,), (0,)), ((), ())), preferred_element_type=jnp.float32
            )
            for k in range(count):
                row = frame * z.rows + first + k
                here = slice(row * z.width, (row + 1) * z.width)
                value = product[k * LANES : k * LANES + z.width] * slope_ref[here, :]
                out_ref[here, :] = value.astype(jnp.bfloat16)


def join_kernel(z, *refs):
    piece_refs, (out_ref, held_ref, sems) = refs[: z.n_time], refs[z.n_time :]
    me = lax.axis_index("tm")
    whole, tail = divmod(TAPS * z.latent, z.piece)

    def each(step, act):
        place = me ^ step
        start = pl.multiple_of(place * z.piece, z.piece)

        def copy(count):
            source = held_ref.at[step, pl.ds(0, count)]
            act(pltpu.make_async_copy(source, out_ref.at[pl.ds(start, count)], sems.at[step]))

        pl.when(place < whole)(functools.partial(copy, z.piece))
        if tail:
            pl.when(place == whole)(functools.partial(copy, tail))

    for step, ref in enumerate(piece_refs):
        held_ref[step] = ref[...].astype(jnp.float32)
        each(step, lambda copy: copy.start())
    for step in range(z.n_time):
        each(step, lambda copy: copy.wait())


def in_hbm(value):
    return pltpu.with_memory_space_constraint(value, pltpu.HBM)


def exchange(values, axis):
    size = lax.axis_size(axis)
    return [
        lax.ppermute(value, axis, [(i, i ^ step) for i in range(size)])
        for step, value in enumerate(values, 1)
    ]


def coset_sum(values):
    while len(values) > 1:
        half = len(values) // 2
        values = [values[i] + values[i + half] for i in range(half)]
    return values[0]


def shards(latent_grad, features, head_weight):
    n_time, n_rows = lax.axis_size("tm"), lax.axis_size("rows")
    z = Sizes(n_time, n_rows, latent_grad.shape, features.shape)
    params = pltpu.CompilerParams(vmem_limit_bytes=32 * 1024 * 1024)
    f32, bf16 = jnp.float32, jnp.bfloat16
    hbm, vmem = pl.BlockSpec(memory_space=pltpu.HBM), pl.BlockSpec(memory_space=pltpu.VMEM)
    cells = z.grid_rows * z.width
    elements = cells * z.channels
    products = z.cols * z.grid_rows * LANES * z.channels
    flat = features.reshape(cells, z.channels)
    tokens = latent_grad.T
    arrived = exchange([tokens] * (n_time - 1), "tm")
    sort, place = sort_rows(z), place_lanes(z)
    act, slope, sort, place, tokens = pl.pallas_call(
        functools.partial(prepare_kernel, z),
        out_shape=[
            jax.ShapeDtypeStruct((z.grid_rows * LANES, z.channels), bf16),
            jax.ShapeDtypeStruct((cells, z.channels), f32),
            jax.ShapeDtypeStruct(sort.shape, bf16),
            jax.ShapeDtypeStruct(place.shape, bf16),
            jax.ShapeDtypeStruct(tokens.shape, bf16),
        ],
        in_specs=[hbm] * 4,
        out_specs=[vmem] * 5,
        scratch_shapes=[pltpu.VMEM((cells, z.channels), bf16), pltpu.SemaphoreType.DMA((3 + z.frames,))],
        compiler_params=params,
        cost_estimate=pl.CostEstimate(
            flops=10 * elements, bytes_accessed=9 * elements, transcendentals=elements
        ),
        name="act_and_slope",
    )(in_hbm(flat), in_hbm(sort), in_hbm(place), in_hbm(tokens))
    windows = pl.pallas_call(
        functools.partial(window_kernel, z),
        out_shape=[jax.ShapeDtypeStruct((n_time, z.frames_x * z.feat, LANES), bf16)] * n_rows,
        compiler_params=params,
        name="latent_windows",
    )(tokens, *arrived)
    arrived = exchange(windows[1:], "rows")
    moved = [windows[0]] + [arrived[step - 1] for step in last_first(n_rows)]
    outs = pl.pallas_call(
        functools.partial(weight_kernel, z),
        out_shape=[jax.ShapeDtypeStruct((z.piece, z.channels), bf16)] * (n_time - 1)
        + [jax.ShapeDtypeStruct((z.cols, z.rows * LANES), bf16)] * z.frames,
        scratch_shapes=[pltpu.VMEM((n_rows * z.frames_x * z.feat, n_time * LANES), bf16)],
        compiler_params=params,
        cost_estimate=pl.CostEstimate(flops=2 * products, bytes_accessed=4 * elements, transcendentals=0),
        name="weight_term",
    )(*moved, sort, place, act)
    pieces, cols = outs[: n_time - 1], outs[n_time - 1 :]
    arrived = exchange(pieces, "tm")
    own = pl.pallas_call(
        functools.partial(own_kernel, z),
        out_shape=jax.ShapeDtypeStruct((z.piece, z.channels), f32),
        compiler_params=params,
        cost_estimate=pl.CostEstimate(
            flops=2 * products // n_time, bytes_accessed=2 * elements, transcendentals=0
        ),
        name="own_piece",
    )(*cols, act)
    for step in last_first(n_time):
        own = own + arrived[step - 1].astype(f32)
    mine = own.astype(bf16)
    cols, mine = lax.optimization_barrier((cols, mine))
    grad = pl.pallas_call(
        functools.partial(features_kernel, z),
        out_shape=jax.ShapeDtypeStruct((cells, z.channels), bf16),
        scratch_shapes=[pltpu.VMEM((z.cols, z.channels), bf16)],
        compiler_params=params,
        cost_estimate=pl.CostEstimate(flops=2 * products, bytes_accessed=8 * elements, transcendentals=0),
        name="features_grad",
    )(*cols, slope, head_weight)
    arrived = exchange([mine] * (n_rows - 1), "rows")
    whole = coset_sum([value.astype(f32) for value in [mine] + arrived])
    scale = 1.0 / math.sqrt(cells * n_time * n_rows)
    whole = (whole * scale).astype(bf16)
    whole, grad = lax.optimization_barrier((whole, grad))
    pieces = [whole] + exchange([whole] * (n_time - 1), "tm")
    weight_grad = pl.pallas_call(
        functools.partial(join_kernel, z),
        out_shape=jax.ShapeDtypeStruct((TAPS * z.latent, z.channels), f32),
        in_specs=[vmem] * n_time,
        out_specs=hbm,
        scratch_shapes=[
            pltpu.VMEM((n_time, z.piece, z.channels), f32),
            pltpu.SemaphoreType.DMA((n_time,)),
        ],
        compiler_params=params,
        name="join_pieces",
    )(*pieces)
    return (grad.reshape(features.shape), weight_grad)


def solution(mesh):
    return jax.shard_map(
        shards,
        mesh=mesh,
        in_specs=(P(("dp", "tm"), "rows"), P(("dp", "tm"), "rows", None, None), P()),
        out_specs=(P(("dp", "tm"), "rows", None, None), P("dp", None)),
        check_vma=False,
    )
```

```python
import functools
import math

import jax
import jax.numpy as jnp
import numpy as np
from jax import lax
from jax.experimental import pallas as pl
from jax.experimental.pallas import tpu as pltpu
from jax.sharding import PartitionSpec as P

LANES = 128
TAPS = 27


class Sizes:
    def __init__(self, n_time, n_rows, latent_shape, features_shape):
        self.n_time, self.n_rows = n_time, n_rows
        self.frames, self.rows, self.width, self.channels = features_shape
        self.tokens, self.feat = latent_shape
        self.latent = self.feat * n_rows // 4
        self.cycle = 2 * n_time
        self.row_tokens = self.width // 2
        self.band = self.rows // 2
        self.band_x = self.band + 2
        self.frames_x = self.frames + 2
        self.all_frames = self.frames * n_time
        self.band_cycles = self.band * self.row_tokens // self.cycle
        self.halo_cycles = -(-self.row_tokens // self.cycle)
        self.halo = 2 * self.halo_cycles
        self.lanes = 2 * self.band_cycles + 2 * self.halo
        self.sources = n_time * n_rows
        self.grid_rows = self.frames * self.rows
        self.piece_taps = -(-TAPS // n_time)
        self.piece = self.piece_taps * self.latent
        self.cols = self.piece * n_time


def sort_rows(z):
    count = z.n_rows * z.frames_x * z.feat
    out = np.zeros((count, count), np.float32)
    part = z.feat // 4
    for r in range(z.n_rows):
        for t in range(z.frames_x):
            for e in range(part):
                for p in range(2):
                    for q in range(2):
                        source = (r * z.frames_x + t) * z.feat + 4 * e + 2 * p + q
                        target = ((q * 2 + p) * z.frames_x + t) * z.latent + r * part + e
                        out[target, source] = 1
    return jnp.asarray(out, jnp.bfloat16)


def place_lanes(z):
    out = np.zeros((2, z.n_time, LANES, z.band_x, LANES), np.float32)
    for q in range(2):
        for i in range(z.n_time):
            for lane in range(z.lanes):
                place = z.cycle - 1 - i if lane % 2 else i
                token = (lane // 2 - z.halo_cycles) * z.cycle + place + z.row_tokens
                if 0 <= token < z.band_x * z.row_tokens:
                    out[q, i, lane, token // z.row_tokens, 2 * (token % z.row_tokens) + q] = 1
    return jnp.asarray(out.reshape(2 * z.n_time * LANES, z.band_x * LANES), jnp.bfloat16)


def window_kernel(z, *refs):
    token_refs, out_refs = refs[: z.n_time], refs[z.n_time :]
    time, band = lax.axis_index("tm"), lax.axis_index("rows")
    lane = lax.broadcasted_iota(jnp.int32, (z.feat, LANES), 1)
    last = z.tokens // LANES - 2
    for step, out_ref in enumerate(out_refs):
        r = band ^ step
        low = jnp.where(r == 0, z.halo, 0)
        high = jnp.where(r == z.n_rows - 1, z.lanes - z.halo, z.lanes)
        inside = (lane >= low) & (lane < high)
        blocks = [[] for _ in token_refs]
        for t in range(z.frames_x):
            frame = time * z.frames + t
            start = 2 * (frame * z.n_rows + r) * z.band_cycles - z.halo
            tile = jnp.clip(start >> 7, 0, last)
            turn = (2 * LANES - (start - tile * LANES)) & (2 * LANES - 1)
            kept = inside & (frame < z.all_frames)
            for ref, held in zip(token_refs, blocks):
                value = ref[:, pl.ds(pl.multiple_of(tile * LANES, LANES), 2 * LANES)]
                value = pltpu.roll(value.astype(jnp.float32), turn, 1)[:, :LANES]
                held.append(jnp.where(kept, value, 0.0))
        for i, held in enumerate(blocks):
            out_ref[time ^ i] = jnp.concatenate(held, axis=0).astype(jnp.bfloat16)


def prepare_kernel(
    z, features_ref, sort_ref, place_ref, tokens_ref, act_ref, slope_ref, sort_out, place_out, tokens_out, held_ref, sems
):
    cells = z.rows * z.width
    frames = [slice(t * cells, (t + 1) * cells) for t in range(z.frames)]
    loads = [
        pltpu.make_async_copy(features_ref.at[here], held_ref.at[here], sems.at[3 + t])
        for t, here in enumerate(frames)
    ]
    copies = [
        pltpu.make_async_copy(sort_ref, sort_out, sems.at[0]),
        pltpu.make_async_copy(place_ref, place_out, sems.at[1]),
        pltpu.make_async_copy(tokens_ref, tokens_out, sems.at[2]),
    ]
    for copy in loads + copies:
        copy.start()
    for row in range(z.grid_rows):
        if row % z.rows == 0:
            loads[row // z.rows].wait()
        here = slice(row * z.width, (row + 1) * z.width)
        hidden = held_ref[here, :].astype(jnp.float32)
        sig = 0.5 + 0.5 * jnp.tanh(0.5 * hidden)
        act = hidden * sig
        act_ref[row * LANES : row * LANES + z.width, :] = act.astype(jnp.bfloat16)
        shape = (LANES - z.width, z.channels)
        act_ref[row * LANES + z.width : (row + 1) * LANES, :] = jnp.zeros(shape, jnp.bfloat16)
        slope_ref[here, :] = sig * (1.0 + hidden * (1.0 - sig))
    for copy in copies:
        copy.wait()


def slot_start(z, piece):
    return pl.multiple_of((lax.axis_index("tm") ^ piece) * z.piece, z.piece)


def last_first(count):
    return [count - 1, *range(1, count - 1)]


def turned_grid(z, moved_refs, sort_ref, place_ref, held_ref):
    count = z.frames_x * z.feat
    rows = z.n_rows * count
    band = lax.axis_index("rows")
    for step, ref in zip([0] + last_first(z.n_rows), moved_refs):
        start = pl.multiple_of((band ^ step) * count, count)
        for i in range(z.n_time):
            held_ref[pl.ds(start, count), i * LANES : (i + 1) * LANES] = ref[i]
    ordered = jnp.dot(
        sort_ref[...], held_ref[...], preferred_element_type=jnp.float32
    ).astype(jnp.bfloat16)
    half = rows // 2
    pair = jnp.concatenate([ordered[:half], ordered[half:]], axis=1)
    grid = jnp.dot(pair, place_ref[...], preferred_element_type=jnp.float32)
    turned = {}
    for a in range(z.band_x):
        block = grid[:, a * LANES : (a + 1) * LANES]
        for kw, turn in enumerate((LANES - 1, 0, 1)):
            value = pltpu.roll(block, turn, 1) if turn else block
            turned[a, kw] = value.astype(jnp.bfloat16)
    return turned


def fill_cols(z, turned, frame, cols_ref, me=None):
    for tap in range(z.n_time * z.piece_taps):
        if me is None:
            start = slot_start(z, tap // z.piece_taps) + tap % z.piece_taps * z.latent
            here = pl.ds(pl.multiple_of(start, z.latent), z.latent)
        else:
            start = (tap // z.piece_taps ^ me) * z.piece + tap % z.piece_taps * z.latent
            here = slice(start, start + z.latent)
        if tap >= TAPS:
            cols_ref[here, :] = jnp.zeros((z.latent, z.rows * LANES), jnp.bfloat16)
            continue
        kt, kh, kw = tap // 9, tap // 3 % 3, tap % 3
        t = frame + 2 - kt
        for row in range(z.rows):
            a, p = divmod(row + 1 - kh + 2, 2)
            at = (p * z.frames_x + t) * z.latent
            cols_ref[here, row * LANES : (row + 1) * LANES] = turned[a, kw][at : at + z.latent]


def weight_kernel(z, *refs):
    moved_refs, (sort_ref, place_ref, act_ref) = refs[: z.n_rows], refs[z.n_rows : z.n_rows + 3]
    out_refs, cols_refs, held_ref = refs[z.n_rows + 3 : -1 - z.frames], refs[-1 - z.frames : -1], refs[-1]

    def term(me=None):
        turned = turned_grid(z, moved_refs, sort_ref, place_ref, held_ref)
        total = 0.0
        for frame, cols_ref in enumerate(cols_refs):
            fill_cols(z, turned, frame, cols_ref, me)
            act = act_ref[frame * z.rows * LANES : (frame + 1) * z.rows * LANES, :]
            total = total + jnp.dot(cols_ref[z.piece :, :], act, preferred_element_type=jnp.float32)
        for step, ref in enumerate(out_refs):
            ref[...] = total[step * z.piece : (step + 1) * z.piece].astype(jnp.bfloat16)

    if z.n_time > 4:
        term()
        return
    for me in range(z.n_time):
        pl.when(lax.axis_index("tm") == me)(functools.partial(term, me))


def own_kernel(z, *refs):
    cols_refs, (act_ref, out_ref) = refs[: z.frames], refs[z.frames :]
    total = 0.0
    for frame, cols_ref in enumerate(cols_refs):
        act = act_ref[frame * z.rows * LANES : (frame + 1) * z.rows * LANES, :]
        total = total + jnp.dot(cols_ref[: z.piece, :], act, preferred_element_type=jnp.float32)
    out_ref[...] = total


def features_kernel(z, *refs):
    cols_refs, (slope_ref, weight_ref, out_ref, held_ref) = refs[: z.frames], refs[z.frames :]
    for piece in range(z.n_time):
        first = piece * z.piece
        count = max(0, min(z.piece, TAPS * z.latent - first))
        start = slot_start(z, piece)
        if count:
            held_ref[pl.ds(start, count), :] = weight_ref[first : first + count, :]
        if count < z.piece:
            start = pl.multiple_of(start + count, z.latent)
            held_ref[pl.ds(start, z.piece - count), :] = jnp.zeros((z.piece - count, z.channels), jnp.bfloat16)
    step = 4
    for frame, cols_ref in enumerate(cols_refs):
        for first in range(0, z.rows, step):
            count = min(step, z.rows - first)
            part = cols_ref[:, first * LANES : (first + count) * LANES]
            product = lax.dot_general(
                part, held_ref[...], (((0,), (0,)), ((), ())), preferred_element_type=jnp.float32
            )
            for k in range(count):
                row = frame * z.rows + first + k
                here = slice(row * z.width, (row + 1) * z.width)
                value = product[k * LANES : k * LANES + z.width] * slope_ref[here, :]
                out_ref[here, :] = value.astype(jnp.bfloat16)


def join_kernel(z, *refs):
    piece_refs, (out_ref, held_ref, sems) = refs[: z.n_time], refs[z.n_time :]
    me = lax.axis_index("tm")
    whole, tail = divmod(TAPS * z.latent, z.piece)

    def each(step, act):
        place = me ^ step
        start = pl.multiple_of(place * z.piece, z.piece)

        def copy(count):
            source = held_ref.at[step, pl.ds(0, count)]
            act(pltpu.make_async_copy(source, out_ref.at[pl.ds(start, count)], sems.at[step]))

        pl.when(place < whole)(functools.partial(copy, z.piece))
        if tail:
            pl.when(place == whole)(functools.partial(copy, tail))

    def fixed(index):
        copies = []
        for step, ref in enumerate(piece_refs):
            held_ref[step] = ref[...].astype(jnp.float32)
            first = (index ^ step) * z.piece
            count = max(0, min(z.piece, TAPS * z.latent - first))
            if count:
                source, target = held_ref.at[step, pl.ds(0, count)], out_ref.at[pl.ds(first, count)]
                copies.append(pltpu.make_async_copy(source, target, sems.at[step]))
                copies[-1].start()
        for copy in copies:
            copy.wait()

    if z.n_time <= 4:
        for index in range(z.n_time):
            pl.when(me == index)(functools.partial(fixed, index))
        return
    for step, ref in enumerate(piece_refs):
        held_ref[step] = ref[...].astype(jnp.float32)
        each(step, lambda copy: copy.start())
    for step in range(z.n_time):
        each(step, lambda copy: copy.wait())


def in_hbm(value):
    return pltpu.with_memory_space_constraint(value, pltpu.HBM)


def exchange(values, axis):
    size = lax.axis_size(axis)
    return [
        lax.ppermute(value, axis, [(i, i ^ step) for i in range(size)])
        for step, value in enumerate(values, 1)
    ]


def coset_sum(values):
    while len(values) > 1:
        half = len(values) // 2
        values = [values[i] + values[i + half] for i in range(half)]
    return values[0]


def shards(latent_grad, features, head_weight):
    n_time, n_rows = lax.axis_size("tm"), lax.axis_size("rows")
    z = Sizes(n_time, n_rows, latent_grad.shape, features.shape)
    params = pltpu.CompilerParams(vmem_limit_bytes=32 * 1024 * 1024)
    f32, bf16 = jnp.float32, jnp.bfloat16
    hbm, vmem = pl.BlockSpec(memory_space=pltpu.HBM), pl.BlockSpec(memory_space=pltpu.VMEM)
    cells = z.grid_rows * z.width
    elements = cells * z.channels
    products = z.cols * z.grid_rows * LANES * z.channels
    flat = features.reshape(cells, z.channels)
    tokens = latent_grad.T
    arrived = exchange([tokens] * (n_time - 1), "tm")
    sort, place = sort_rows(z), place_lanes(z)
    act, slope, sort, place, tokens = pl.pallas_call(
        functools.partial(prepare_kernel, z),
        out_shape=[
            jax.ShapeDtypeStruct((z.grid_rows * LANES, z.channels), bf16),
            jax.ShapeDtypeStruct((cells, z.channels), f32),
            jax.ShapeDtypeStruct(sort.shape, bf16),
            jax.ShapeDtypeStruct(place.shape, bf16),
            jax.ShapeDtypeStruct(tokens.shape, bf16),
        ],
        in_specs=[hbm] * 4,
        out_specs=[vmem] * 5,
        scratch_shapes=[pltpu.VMEM((cells, z.channels), bf16), pltpu.SemaphoreType.DMA((3 + z.frames,))],
        compiler_params=params,
        cost_estimate=pl.CostEstimate(
            flops=10 * elements, bytes_accessed=9 * elements, transcendentals=elements
        ),
        name="act_and_slope",
    )(in_hbm(flat), in_hbm(sort), in_hbm(place), in_hbm(tokens))
    windows = pl.pallas_call(
        functools.partial(window_kernel, z),
        out_shape=[jax.ShapeDtypeStruct((n_time, z.frames_x * z.feat, LANES), bf16)] * n_rows,
        compiler_params=params,
        name="latent_windows",
    )(tokens, *arrived)
    arrived = exchange(windows[1:], "rows")
    moved = [windows[0]] + [arrived[step - 1] for step in last_first(n_rows)]
    outs = pl.pallas_call(
        functools.partial(weight_kernel, z),
        out_shape=[jax.ShapeDtypeStruct((z.piece, z.channels), bf16)] * (n_time - 1)
        + [jax.ShapeDtypeStruct((z.cols, z.rows * LANES), bf16)] * z.frames,
        scratch_shapes=[pltpu.VMEM((n_rows * z.frames_x * z.feat, n_time * LANES), bf16)],
        compiler_params=params,
        cost_estimate=pl.CostEstimate(flops=2 * products, bytes_accessed=4 * elements, transcendentals=0),
        name="weight_term",
    )(*moved, sort, place, act)
    pieces, cols = outs[: n_time - 1], outs[n_time - 1 :]
    arrived = exchange(pieces, "tm")
    own = pl.pallas_call(
        functools.partial(own_kernel, z),
        out_shape=jax.ShapeDtypeStruct((z.piece, z.channels), f32),
        compiler_params=params,
        cost_estimate=pl.CostEstimate(
            flops=2 * products // n_time, bytes_accessed=2 * elements, transcendentals=0
        ),
        name="own_piece",
    )(*cols, act)
    for step in last_first(n_time):
        own = own + arrived[step - 1].astype(f32)
    mine = own.astype(bf16)
    cols, mine = lax.optimization_barrier((cols, mine))
    grad = pl.pallas_call(
        functools.partial(features_kernel, z),
        out_shape=jax.ShapeDtypeStruct((cells, z.channels), bf16),
        scratch_shapes=[pltpu.VMEM((z.cols, z.channels), bf16)],
        compiler_params=params,
        cost_estimate=pl.CostEstimate(flops=2 * products, bytes_accessed=8 * elements, transcendentals=0),
        name="features_grad",
    )(*cols, slope, head_weight)
    arrived = exchange([mine] * (n_rows - 1), "rows")
    whole = coset_sum([value.astype(f32) for value in [mine] + arrived])
    scale = 1.0 / math.sqrt(cells * n_time * n_rows)
    whole = (whole * scale).astype(bf16)
    whole, grad = lax.optimization_barrier((whole, grad))
    pieces = [whole] + exchange([whole] * (n_time - 1), "tm")
    weight_grad = pl.pallas_call(
        functools.partial(join_kernel, z),
        out_shape=jax.ShapeDtypeStruct((TAPS * z.latent, z.channels), f32),
        in_specs=[vmem] * n_time,
        out_specs=hbm,
        scratch_shapes=[
            pltpu.VMEM((n_time, z.piece, z.channels), f32),
            pltpu.SemaphoreType.DMA((n_time,)),
        ],
        compiler_params=params,
        name="join_pieces",
    )(*pieces)
    return (grad.reshape(features.shape), weight_grad)


def solution(mesh):
    return jax.shard_map(
        shards,
        mesh=mesh,
        in_specs=(P(("dp", "tm"), "rows"), P(("dp", "tm"), "rows", None, None), P()),
        out_specs=(P(("dp", "tm"), "rows", None, None), P("dp", None)),
        check_vma=False,
    )
```
